32 devices in a mesh: parts: 2 (over y), feat: 4 (over z), store: 4 (over x, core).
Axes of the slice: x: 2, y: 2, z: 4, core: 2. Of those that a mesh axis runs over, the one named last changes fastest.
Arguments:
- queries: bfloat16 [8192, 65536], P(('parts', 'store'), 'feat'), parts along dimension 0, may hold values from -6 to 6
- store_rows: bfloat16 [4096, 65536], P(('parts', 'store'), 'feat'), parts along dimension 0, may hold values from -0.03125 to 0.03125
- feature_scale: float32 [65536], P('feat'), may hold values from 0.1 to 10
Outputs:
- scores: float32 [2048, 8192], P('feat', ('parts', 'store')), parts along dimension 1
The draws below stay inside these ranges and needn't reach their ends.
There are 2 independent parts, one for each index of `parts`. The reference program is written for one: setup_inputs(seed, part) draws one part's arguments, and reference() takes and returns one part's arrays. A program takes and returns all parts, laid end to end along the dimension named above; an argument that names none is the same for every part. Nothing has to cross between parts.
All inputs are finite; a program needn't handle non-finite values.
Results may differ from the reference program's by a relative error of at most 0.0029.
Values may be sent and summed in bfloat16 or wider, within the bound.
A program may use at most 256 MiB of HBM per device.

```python
import math
import jax
import jax.numpy as jnp

F = 65536
QUERIES = 4096
WINDOW = 2048


def with_spikes(drawn, rng, source, target, shards_of, factor):
    owner, partner = [(jnp.arange(drawn.shape[axis_at]) // (drawn.shape[axis_at] // shards_of)).reshape([-1 if axis == axis_at else 1 for axis in range(drawn.ndim)]) for axis_at in (source, target)]
    chosen = jax.random.permutation(rng, shards_of)[partner]
    strong = (owner == chosen) | (owner == (partner + shards_of // 2) % shards_of)
    return jnp.where(strong, factor * drawn, drawn)


def block_levels(key, extent, pieces, least, largest):
    def one(position, blocks):
        steps = jax.random.uniform(jax.random.fold_in(jax.random.fold_in(key, 6), position), (blocks,), jnp.float32, least / len(pieces), largest / len(pieces))
        return jnp.repeat(jnp.exp(steps), extent[position] // blocks).reshape((-1,) + (1,) * (len(extent) - position - 1))

    loudness = one(*pieces[0])
    for cut in pieces[1:]:
        loudness = loudness * one(*cut)
    return loudness


def gaussian(key, dims, deviation, bound, split=(), dtype=jnp.bfloat16):
    values = jax.random.normal(key, dims, jnp.float32) * deviation
    if len(split) > 0:
        values = block_levels(key, dims, split, -0.22, 0.18) * values
    return jnp.clip(values, min=-bound, max=bound).astype(dtype)


def bell_draw_with(stream_key, extent, spread, reach, cuts, heavy, dtype=jnp.bfloat16):
    result = spread * jax.random.normal(stream_key, extent, jnp.float32)
    if cuts:
        result = result * block_levels(stream_key, extent, cuts, -0.22, 0.18)
    return jnp.clip(with_spikes(result, jax.random.fold_in(stream_key, 3), *heavy), -reach, reach).astype(dtype)


def setup_inputs(seed: int = 0, part: int = 0) -> dict:
    streams_of = jax.random.split(jax.random.key(seed), 4)
    part_keys = jax.random.split(jax.random.fold_in(streams_of[3], part), 4)
    queries = gaussian(part_keys[0], (QUERIES, F), 1.0, 6.0, ((0, 4), (1, 4)))
    store_rows = bell_draw_with(part_keys[1], (WINDOW, F), F ** -0.5, 0.03125, ((0, 4), (1, 4)), (1, 0, 4, 2.0))
    feature_scale = jnp.clip(jnp.exp(math.log(10.0) - 4.6051702 * jax.random.uniform(streams_of[2], (F,), jnp.float32) ** block_levels(streams_of[2], (F,), ((0, 4),), -0.2, 0.2)), 0.1, 10.0)
    return {"queries": queries, "store_rows": store_rows, "feature_scale": feature_scale}


def reference(queries, store_rows, feature_scale):
    scaled = (queries.astype(jnp.float32) * feature_scale[None, :]).astype(jnp.bfloat16)
    return jnp.dot(store_rows, scaled.T, preferred_element_type=jnp.float32)
```

```python
import functools

import jax
import jax.numpy as jnp
from jax import lax
from jax.experimental import pallas as pl
from jax.experimental.pallas import tpu as pltpu
from jax.sharding import PartitionSpec as P

MESH = pl.DeviceIdType.MESH
EARLY_ROWS = 128
LATE_ROWS = 32
PIECE = 4096
AHEAD = 4
BURST = 16
SLOTS = 4
NT = 256


def kernel(n_feat, cfg, queries, store, scale, out, got, q, stage, acc_e, acc_l, recv,
           q_sem, load_sem, sib_send, sib_recv, x_send, x_recv, relay_send, relay_recv,
           red_send_e, red_recv_e, red_send_l, red_recv_l):
    W, K, NQ, share, Re, Rl, Kp, QR = cfg
    nk = K // Kp
    n_early, n_late = W // Re, W // Rl
    pieces_e, pieces = n_early * nk, n_late * nk
    s = lax.axis_index("store")
    me = lax.axis_index("feat")
    sib = s + 1 - 2 * lax.rem(s, 2)
    partner = lax.rem(s + 2, 4)
    far = lax.rem(sib + 2, 4)

    def q_copy(i):
        rows = pl.ds(pl.multiple_of(i * QR, QR), QR)
        return pltpu.make_async_copy(queries.at[rows], q.at[rows], q_sem.at[i])

    def sib_copy(c):
        rows = pl.ds(pl.multiple_of(c * Re, Re), Re)
        return pltpu.make_async_remote_copy(
            store.at[rows], got.at[0, rows], sib_send.at[c], sib_recv.at[c],
            device_id={"store": sib}, device_id_type=MESH)

    def where(p):
        return (pl.ds(pl.multiple_of((p // nk) * Rl, Rl), Rl),
                pl.ds(pl.multiple_of((p % nk) * Kp, Kp), Kp))

    def x_copy(p):
        rows, cols = where(p)
        return pltpu.make_async_remote_copy(
            store.at[rows, cols], got.at[1, rows, cols], x_send.at[p], x_recv.at[p],
            device_id={"store": partner}, device_id_type=MESH)

    def relay_copy(p):
        rows, cols = where(p)
        return pltpu.make_async_remote_copy(
            got.at[1, rows, cols], got.at[2, rows, cols], relay_send.at[p], relay_recv.at[p],
            device_id={"store": sib}, device_id_type=MESH)

    def load_late(p, half):
        rows, cols = where(p)
        slot = lax.rem(p, 2)
        return pltpu.make_async_copy(
            got.at[1 + half, rows, cols], stage.at[slot, pl.ds(half * Rl, Rl)],
            load_sem.at[slot, half])

    def load_early(p, half):
        rows = pl.ds(pl.multiple_of((p // nk) * Re, Re), Re)
        cols = pl.ds(pl.multiple_of((p % nk) * Kp, Kp), Kp)
        slot = lax.rem(p, 2)
        src = store.at[rows, cols] if half == 0 else got.at[0, rows, cols]
        return pltpu.make_async_copy(
            src, stage.at[slot, pl.ds(half * Re, Re)], load_sem.at[slot, half])

    barrier = pltpu.get_barrier_semaphore()
    for target in (sib, partner):
        pl.semaphore_signal(barrier, inc=1, device_id={"store": target}, device_id_type=MESH)

    @pl.loop(1, n_feat)
    def _(d):
        pl.semaphore_signal(barrier, inc=1, device_id={"feat": lax.rem(me + d, n_feat)},
                            device_id_type=MESH)

    @pl.loop(0, NQ // QR)
    def _(i):
        q_copy(i).start()

    load_early(0, 0).start()
    pl.semaphore_wait(barrier, n_feat + 1)

    burst = min(BURST, pieces)

    @pl.loop(0, burst)
    def _(p):
        x_copy(p).start()

    @pl.loop(0, n_early)
    def _(c):
        sib_copy(c).start()

    @pl.loop(0, NQ // QR)
    def _(i):
        q_copy(i).wait()

        @pl.loop(0, QR // 16)
        def _(j):
            rows = pl.ds(pl.multiple_of(i * QR + j * 16, 16), 16)
            for k0 in range(0, K, 2048):
                part = q[rows, k0:k0 + 2048].astype(jnp.float32) * scale[:, k0:k0 + 2048]
                q[rows, k0:k0 + 2048] = part.astype(jnp.bfloat16)

    def multiply(acc, p, R):
        slot = lax.rem(p, 2)
        k = lax.rem(p, nk)
        cols = pl.ds(pl.multiple_of(k * Kp, Kp), Kp)

        @pl.when(k == 0)
        def _():
            acc[...] = jnp.zeros(acc.shape, jnp.float32)

        for n0 in range(0, NQ, NT):
            acc[:, n0:n0 + NT] += lax.dot_general(
                stage[slot, :2 * R], q[n0:n0 + NT, cols], (((1,), (1,)), ((), ())),
                preferred_element_type=jnp.float32)

    def half_at(block, c, R):
        row = block * W + c * R
        return row // share, lax.rem(row, share)

    def send(acc, block, c, R, half, send_sem, recv_sem):
        t, off = half_at(block, c, R)
        return t, off, pltpu.make_async_remote_copy(
            acc.at[pl.ds(half * R, R)], recv.at[me, pl.ds(pl.multiple_of(off, R), R)],
            send_sem, recv_sem.at[me, off // R],
            device_id={"feat": t}, device_id_type=MESH)

    def hand_on(acc, blocks, c, R, send_sems, recv_sem):
        for half in range(2):
            t, off, copy = send(acc, blocks[half], c, R, half, send_sems.at[half], recv_sem)

            @pl.when(t == me)
            def _():
                recv[me, pl.ds(pl.multiple_of(off, R), R)] = acc[half * R:(half + 1) * R]

            @pl.when(t != me)
            def _():
                copy.start()

    def wait_sent(acc, blocks, c, R, send_sems, recv_sem):
        for half in range(2):
            t, off, copy = send(acc, blocks[half], c, R, half, send_sems.at[half], recv_sem)

            @pl.when(t != me)
            def _():
                copy.wait_send()

    def collect(blocks, c, R, recv_sem):
        for half in range(2):
            t, off = half_at(blocks[half], c, R)

            @pl.when(t == me)
            def _():
                rows = pl.ds(pl.multiple_of(off, R), R)

                @pl.loop(1, n_feat)
                def _(d):
                    f = lax.rem(me + d, n_feat)
                    pltpu.make_async_copy(
                        recv.at[f, rows], recv.at[f, rows], recv_sem.at[f, off // R]).wait()

                total = recv[0, rows]
                for f in range(1, n_feat):
                    total = total + recv[f, rows]
                out[rows] = total

    early, late = (s, sib), (partner, far)

    sib_copy(0).wait_recv()
    load_early(0, 1).start()

    @pl.loop(0, pieces_e)
    def _(p):
        @pl.when(p + 1 < pieces_e)
        def _():
            load_early(p + 1, 0).start()

            @pl.when(lax.rem(p + 1, nk) == 0)
            def _():
                sib_copy((p + 1) // nk).wait_recv()

            load_early(p + 1, 1).start()

        for half in range(2):
            load_early(p, half).wait()
        c = p // nk
        multiply(acc_e.at[c], p, Re)

        @pl.when(lax.rem(p, nk) == nk - 1)
        def _():
            hand_on(acc_e.at[c], early, c, Re, red_send_e.at[c], red_recv_e)

    def front(p):
        x_copy(p).wait_recv()
        relay_copy(p).start()
        load_late(p, 0).start()
        x_copy(p).wait_send()

        @pl.when((p + AHEAD >= burst) & (p + AHEAD < pieces))
        def _():
            x_copy(p + AHEAD).start()

    def mid(p):
        relay_copy(p).wait_recv()
        load_late(p, 1).start()

    front(0)
    mid(0)

    @pl.loop(0, pieces)
    def _(p):
        c = p // nk
        k = lax.rem(p, nk)
        slot = lax.rem(c, SLOTS)

        @pl.when(p + 1 < pieces)
        def _():
            front(p + 1)

        @pl.when((k == 0) & (c >= SLOTS))
        def _():
            wait_sent(acc_l.at[slot], late, c - SLOTS, Rl, red_send_l.at[slot], red_recv_l)

        for half in range(2):
            load_late(p, half).wait()
        multiply(acc_l.at[slot], p, Rl)

        @pl.when(k == nk - 1)
        def _():
            hand_on(acc_l.at[slot], late, c, Rl, red_send_l.at[slot], red_recv_l)

        @pl.when(p + 1 < pieces)
        def _():
            mid(p + 1)

        @pl.when((k == nk - 1) & (c >= 2))
        def _():
            collect(late, c - 2, Rl, red_recv_l)

        @pl.when((k == nk - 1) & (c == (3 * n_late) // 4))
        def _():
            @pl.loop(0, n_early)
            def _(e):
                collect(early, e, Re, red_recv_e)

    for c in range(max(n_late - 2, 0), n_late):
        collect(late, c, Rl, red_recv_l)

    @pl.loop(0, n_early)
    def _(c):
        sib_copy(c).wait_send()
        wait_sent(acc_e.at[c], early, c, Re, red_send_e.at[c], red_recv_e)

    @pl.loop(0, pieces)
    def _(p):
        relay_copy(p).wait_send()

    for c in range(max(n_late - SLOTS, 0), n_late):
        wait_sent(acc_l.at[c % SLOTS], late, c, Rl, red_send_l.at[c % SLOTS], red_recv_l)


def solution(mesh):
    n_feat = mesh.shape["feat"]
    members = mesh.shape["store"]
    assert members == 4

    def local(queries, store_rows, feature_scale):
        NQ, K = queries.shape
        W = store_rows.shape[0]
        share = W * members // n_feat
        Re, Rl = min(EARLY_ROWS, share, W), min(LATE_ROWS, share, W)
        Kp = min(PIECE, K)
        QR = min(128, NQ)
        nk, n_early, n_late = K // Kp, W // Re, W // Rl
        pieces = n_late * nk
        any_space = pl.BlockSpec(memory_space=pl.ANY)
        vmem = pl.BlockSpec(memory_space=pltpu.VMEM)
        dma = pltpu.SemaphoreType.DMA
        result, _ = pl.pallas_call(
            functools.partial(kernel, n_feat, (W, K, NQ, share, Re, Rl, Kp, QR)),
            out_shape=(jax.ShapeDtypeStruct((share, NQ), jnp.float32),
                       jax.ShapeDtypeStruct((3, W, K), jnp.bfloat16)),
            in_specs=[any_space, any_space, vmem],
            out_specs=(vmem, any_space),
            scratch_shapes=[
                pltpu.VMEM((NQ, K), jnp.bfloat16),
                pltpu.VMEM((2, 2 * Re, Kp), jnp.bfloat16),
                pltpu.VMEM((n_early, 2 * Re, NQ), jnp.float32),
                pltpu.VMEM((SLOTS, 2 * Rl, NQ), jnp.float32),
                pltpu.VMEM((n_feat, share, NQ), jnp.float32),
                dma((NQ // QR,)), dma((2, 2)),
                dma((n_early,)), dma((n_early,)),
                dma((pieces,)), dma((pieces,)), dma((pieces,)), dma((pieces,)),
                dma((n_early, 2)), dma((n_feat, share // Re)),
                dma((SLOTS, 2)), dma((n_feat, share // Rl)),
            ],
            compiler_params=pltpu.CompilerParams(
                collective_id=0, has_side_effects=True, vmem_limit_bytes=58 * 2**20),
            cost_estimate=pl.CostEstimate(
                flops=2 * W * members * NQ * K, bytes_accessed=2 * K * (NQ + 7 * W),
                transcendentals=0),
        )(queries, store_rows, feature_scale.reshape(1, K))
        return result

    return jax.shard_map(
        local,
        mesh=mesh,
        in_specs=(P(("parts", "store"), "feat"), P(("parts", "store"), "feat"), P("feat")),
        out_specs=P("feat", ("parts", "store")),
        check_vma=False,
    )
```

```python
import functools

import jax
import jax.numpy as jnp
from jax import lax
from jax.experimental import pallas as pl
from jax.experimental.pallas import tpu as pltpu
from jax.sharding import PartitionSpec as P

MESH = pl.DeviceIdType.MESH
EARLY_ROWS = 128
LATE_ROWS = 32
PIECE = 4096
AHEAD = 8
BURST = 16
SLOTS = 4
NT = 256


def kernel(n_feat, cfg, queries, store, scale, out, got, q, stage, acc_e, acc_l, recv,
           q_sem, load_sem, sib_send, sib_recv, x_send, x_recv, relay_send, relay_recv,
           red_send_e, red_recv_e, red_send_l, red_recv_l):
    W, K, NQ, share, Re, Rl, Kp, QR = cfg
    nk = K // Kp
    n_early, n_late = W // Re, W // Rl
    pieces_e, pieces = n_early * nk, n_late * nk
    s = lax.axis_index("store")
    me = lax.axis_index("feat")
    sib = s + 1 - 2 * lax.rem(s, 2)
    partner = lax.rem(s + 2, 4)
    far = lax.rem(sib + 2, 4)

    def q_copy(i):
        rows = pl.ds(pl.multiple_of(i * QR, QR), QR)
        return pltpu.make_async_copy(queries.at[rows], q.at[rows], q_sem.at[i])

    def sib_copy(c):
        rows = pl.ds(pl.multiple_of(c * Re, Re), Re)
        return pltpu.make_async_remote_copy(
            store.at[rows], got.at[0, rows], sib_send.at[c], sib_recv.at[c],
            device_id={"store": sib}, device_id_type=MESH)

    def where(p):
        return (pl.ds(pl.multiple_of((p // nk) * Rl, Rl), Rl),
                pl.ds(pl.multiple_of((p % nk) * Kp, Kp), Kp))

    def x_copy(p):
        rows, cols = where(p)
        return pltpu.make_async_remote_copy(
            store.at[rows, cols], got.at[1, rows, cols], x_send.at[p], x_recv.at[p],
            device_id={"store": partner}, device_id_type=MESH)

    def relay_copy(p):
        rows, cols = where(p)
        return pltpu.make_async_remote_copy(
            got.at[1, rows, cols], got.at[2, rows, cols], relay_send.at[p], relay_recv.at[p],
            device_id={"store": sib}, device_id_type=MESH)

    def load_late(p, half):
        rows, cols = where(p)
        slot = lax.rem(p, 2)
        return pltpu.make_async_copy(
            got.at[1 + half, rows, cols], stage.at[slot, pl.ds(half * Rl, Rl)],
            load_sem.at[slot, half])

    def load_early(p, half):
        rows = pl.ds(pl.multiple_of((p // nk) * Re, Re), Re)
        cols = pl.ds(pl.multiple_of((p % nk) * Kp, Kp), Kp)
        slot = lax.rem(p, 2)
        src = store.at[rows, cols] if half == 0 else got.at[0, rows, cols]
        return pltpu.make_async_copy(
            src, stage.at[slot, pl.ds(half * Re, Re)], load_sem.at[slot, half])

    barrier = pltpu.get_barrier_semaphore()
    for target in (sib, partner):
        pl.semaphore_signal(barrier, inc=1, device_id={"store": target}, device_id_type=MESH)

    @pl.loop(1, n_feat)
    def _(d):
        pl.semaphore_signal(barrier, inc=1, device_id={"feat": lax.rem(me + d, n_feat)},
                            device_id_type=MESH)

    @pl.loop(0, NQ // QR)
    def _(i):
        q_copy(i).start()

    load_early(0, 0).start()
    pl.semaphore_wait(barrier, n_feat + 1)

    burst = min(BURST, pieces)

    @pl.loop(0, burst)
    def _(p):
        x_copy(p).start()

    @pl.loop(0, n_early)
    def _(c):
        sib_copy(c).start()

    @pl.loop(0, NQ // QR)
    def _(i):
        q_copy(i).wait()

        @pl.loop(0, QR // 16)
        def _(j):
            rows = pl.ds(pl.multiple_of(i * QR + j * 16, 16), 16)
            for k0 in range(0, K, 2048):
                part = q[rows, k0:k0 + 2048].astype(jnp.float32) * scale[:, k0:k0 + 2048]
                q[rows, k0:k0 + 2048] = part.astype(jnp.bfloat16)

    def multiply(acc, p, R):
        slot = lax.rem(p, 2)
        k = lax.rem(p, nk)
        cols = pl.ds(pl.multiple_of(k * Kp, Kp), Kp)

        @pl.when(k == 0)
        def _():
            acc[...] = jnp.zeros(acc.shape, jnp.float32)

        for n0 in range(0, NQ, NT):
            acc[:, n0:n0 + NT] += lax.dot_general(
                stage[slot, :2 * R], q[n0:n0 + NT, cols], (((1,), (1,)), ((), ())),
                preferred_element_type=jnp.float32)

    def half_at(block, c, R):
        row = block * W + c * R
        return row // share, lax.rem(row, share)

    def send(acc, block, c, R, half, send_sem, recv_sem):
        t, off = half_at(block, c, R)
        return t, off, pltpu.make_async_remote_copy(
            acc.at[pl.ds(half * R, R)], recv.at[me, pl.ds(pl.multiple_of(off, R), R)],
            send_sem, recv_sem.at[me, off // R],
            device_id={"feat": t}, device_id_type=MESH)

    def hand_on(acc, blocks, c, R, send_sems, recv_sem):
        for half in range(2):
            t, off, copy = send(acc, blocks[half], c, R, half, send_sems.at[half], recv_sem)

            @pl.when(t == me)
            def _():
                recv[me, pl.ds(pl.multiple_of(off, R), R)] = acc[half * R:(half + 1) * R]

            @pl.when(t != me)
            def _():
                copy.start()

    def wait_sent(acc, blocks, c, R, send_sems, recv_sem):
        for half in range(2):
            t, off, copy = send(acc, blocks[half], c, R, half, send_sems.at[half], recv_sem)

            @pl.when(t != me)
            def _():
                copy.wait_send()

    def collect(blocks, c, R, recv_sem):
        for half in range(2):
            t, off = half_at(blocks[half], c, R)

            @pl.when(t == me)
            def _():
                rows = pl.ds(pl.multiple_of(off, R), R)

                @pl.loop(1, n_feat)
                def _(d):
                    f = lax.rem(me + d, n_feat)
                    pltpu.make_async_copy(
                        recv.at[f, rows], recv.at[f, rows], recv_sem.at[f, off // R]).wait()

                total = recv[0, rows]
                for f in range(1, n_feat):
                    total = total + recv[f, rows]
                out[rows] = total

    early, late = (s, sib), (partner, far)

    sib_copy(0).wait_recv()
    load_early(0, 1).start()

    @pl.loop(0, pieces_e)
    def _(p):
        @pl.when(p + 1 < pieces_e)
        def _():
            load_early(p + 1, 0).start()

            @pl.when(lax.rem(p + 1, nk) == 0)
            def _():
                sib_copy((p + 1) // nk).wait_recv()

            load_early(p + 1, 1).start()

        for half in range(2):
            load_early(p, half).wait()
        c = p // nk
        multiply(acc_e.at[c], p, Re)

        @pl.when(lax.rem(p, nk) == nk - 1)
        def _():
            hand_on(acc_e.at[c], early, c, Re, red_send_e.at[c], red_recv_e)

    def front(p):
        x_copy(p).wait_recv()
        relay_copy(p).start()
        load_late(p, 0).start()
        x_copy(p).wait_send()

        @pl.when((p + AHEAD >= burst) & (p + AHEAD < pieces))
        def _():
            x_copy(p + AHEAD).start()

    def mid(p):
        relay_copy(p).wait_recv()
        load_late(p, 1).start()

    front(0)
    mid(0)

    @pl.loop(0, pieces)
    def _(p):
        c = p // nk
        k = lax.rem(p, nk)
        slot = lax.rem(c, SLOTS)

        @pl.when(p + 1 < pieces)
        def _():
            front(p + 1)

        @pl.when((k == 0) & (c >= SLOTS))
        def _():
            wait_sent(acc_l.at[slot], late, c - SLOTS, Rl, red_send_l.at[slot], red_recv_l)

        for half in range(2):
            load_late(p, half).wait()
        multiply(acc_l.at[slot], p, Rl)

        @pl.when(k == nk - 1)
        def _():
            hand_on(acc_l.at[slot], late, c, Rl, red_send_l.at[slot], red_recv_l)

        @pl.when(p + 1 < pieces)
        def _():
            mid(p + 1)

        @pl.when((k == nk - 1) & (c >= 2))
        def _():
            collect(late, c - 2, Rl, red_recv_l)

        @pl.when((k == nk - 1) & (c == (3 * n_late) // 4))
        def _():
            @pl.loop(0, n_early)
            def _(e):
                collect(early, e, Re, red_recv_e)

    for c in range(max(n_late - 2, 0), n_late):
        collect(late, c, Rl, red_recv_l)

    @pl.loop(0, n_early)
    def _(c):
        sib_copy(c).wait_send()
        wait_sent(acc_e.at[c], early, c, Re, red_send_e.at[c], red_recv_e)

    @pl.loop(0, pieces)
    def _(p):
        relay_copy(p).wait_send()

    for c in range(max(n_late - SLOTS, 0), n_late):
        wait_sent(acc_l.at[c % SLOTS], late, c, Rl, red_send_l.at[c % SLOTS], red_recv_l)


def solution(mesh):
    n_feat = mesh.shape["feat"]
    members = mesh.shape["store"]
    assert members == 4

    def local(queries, store_rows, feature_scale):
        NQ, K = queries.shape
        W = store_rows.shape[0]
        share = W * members // n_feat
        Re, Rl = min(EARLY_ROWS, share, W), min(LATE_ROWS, share, W)
        Kp = min(PIECE, K)
        QR = min(128, NQ)
        nk, n_early, n_late = K // Kp, W // Re, W // Rl
        pieces = n_late * nk
        any_space = pl.BlockSpec(memory_space=pl.ANY)
        vmem = pl.BlockSpec(memory_space=pltpu.VMEM)
        dma = pltpu.SemaphoreType.DMA
        result, _ = pl.pallas_call(
            functools.partial(kernel, n_feat, (W, K, NQ, share, Re, Rl, Kp, QR)),
            out_shape=(jax.ShapeDtypeStruct((share, NQ), jnp.float32),
                       jax.ShapeDtypeStruct((3, W, K), jnp.bfloat16)),
            in_specs=[any_space, any_space, vmem],
            out_specs=(vmem, any_space),
            scratch_shapes=[
                pltpu.VMEM((NQ, K), jnp.bfloat16),
                pltpu.VMEM((2, 2 * Re, Kp), jnp.bfloat16),
                pltpu.VMEM((n_early, 2 * Re, NQ), jnp.float32),
                pltpu.VMEM((SLOTS, 2 * Rl, NQ), jnp.float32),
                pltpu.VMEM((n_feat, share, NQ), jnp.float32),
                dma((NQ // QR,)), dma((2, 2)),
                dma((n_early,)), dma((n_early,)),
                dma((pieces,)), dma((pieces,)), dma((pieces,)), dma((pieces,)),
                dma((n_early, 2)), dma((n_feat, share // Re)),
                dma((SLOTS, 2)), dma((n_feat, share // Rl)),
            ],
            compiler_params=pltpu.CompilerParams(
                collective_id=0, has_side_effects=True, vmem_limit_bytes=58 * 2**20),
            cost_estimate=pl.CostEstimate(
                flops=2 * W * members * NQ * K, bytes_accessed=2 * K * (NQ + 7 * W),
                transcendentals=0),
        )(queries, store_rows, feature_scale.reshape(1, K))
        return result

    return jax.shard_map(
        local,
        mesh=mesh,
        in_specs=(P(("parts", "store"), "feat"), P(("parts", "store"), "feat"), P("feat")),
        out_specs=P("feat", ("parts", "store")),
        check_vma=False,
    )
```
